32 devices in a mesh: groups: 2 (over y), wide: 16 (over z, x, core).
Axes of the slice: x: 2, y: 2, z: 4, core: 2. Of those that a mesh axis runs over, the one named last changes fastest.
Arguments:
- queries: bfloat16 [2048, 768], P(('groups', 'wide')), parts along dimension 0, may hold values from -6 to 6
- beam_owner: int32 [2048, 4], P(('groups', 'wide')), parts along dimension 0, may hold values from 0 to 15, all different within a row; in each aligned block of 64 rows (0 to 63, 64 to 127, ...) at most 32 rows name the same one
- beam_local: int32 [2048, 8], P(('groups', 'wide')), parts along dimension 0, may hold values from 0 to 127
- leaf_weight: bfloat16 [4096, 16, 768], P(('groups', 'wide')), parts along dimension 0, may hold values from -0.4375 to 0.4375
- leaf_bias: float32 [4096, 16], P(('groups', 'wide')), parts along dimension 0, may hold values from -2 to 2
- cluster_weight: bfloat16 [4096, 768], P(('groups', 'wide')), parts along dimension 0, may hold values from -0.4375 to 0.4375
- block_size: int32 [4096], P(('groups', 'wide')), parts along dimension 0, may hold values from 1 to 16
Outputs:
- label_scores: float32 [2048, 128], P(('groups', 'wide')), parts along dimension 0
The draws below stay inside these ranges and needn't reach their ends.
There are 2 independent parts, one for each index of `groups`. The reference program is written for one: setup_inputs(seed, part) draws one part's arguments, and reference() takes and returns one part's arrays. A program takes and returns all parts, laid end to end along the dimension named above; each array names one. Nothing has to cross between parts.
Inputs may be any that keep to these rules, and one draw needn't show every extreme that they name: `beam_owner`: each query names 4 different devices. Among the rows of one device no device is named more than 32 times, and some device is named exactly 32 times.
All inputs are finite; a program needn't handle non-finite values.
Results may differ from the reference program's by a relative error of at most 0.0003.
Values may be sent and summed in bfloat16 or wider, within the bound.
A program may use at most 64 MiB of HBM per device.

```python
import math
import jax
import jax.numpy as jnp
import numpy as np
from jax import lax

D = 768
B = 16
K = 8
KO = 4
TOK_DEV = 64
CL_DEV = 128
CAP = 32
TOKENS = 1024
LEAFC = 2048
N_WIDE = 16


def plant(entries, key, smallest, high):
    longest = entries.shape.index(max(entries.shape))
    spots = []
    for shift in (0, 1):
        where = [jax.random.randint(jax.random.fold_in(key, axis), (), 0, length) for axis, length in enumerate(entries.shape)]
        where[longest] = (where[longest] + shift) % entries.shape[longest]
        spots.append(tuple(where))
    return entries.at[spots[0]].set(smallest).at[spots[1]].set(high)


def block_levels(key, shape, split, smallest, largest):
    gain, own = 1.0, jax.random.fold_in(key, 6)
    for position, parts in split:
        steps = jnp.exp(jax.random.uniform(jax.random.fold_in(own, position), (parts,), jnp.float32, smallest / len(split), largest / len(split)))
        gain = gain * jnp.repeat(steps, shape[position] // parts).reshape([-1 if axis == position else 1 for axis in range(len(shape))])
    return gain


def shared_out(stream_key, own, number, rows, count, top, limit, slope):
    sequence = jax.random.permutation(stream_key, count)
    heavy_load, common = load_shares(count, rows * top, limit, slope, True), load_shares(count, rows * top, limit, slope, False)
    places = jnp.arange(count)

    def named(lengths, turn):
        used = int((lengths > 0).sum())
        fixed = max(1, used // 4)
        passed = fixed + (places - fixed + turn * (used - fixed)) % max(1, count - fixed)
        return jnp.zeros((count,), jnp.int32).at[sequence[jnp.where(places < fixed, places, passed)]].set(jnp.asarray(lengths, jnp.int32))

    lengths = jnp.where(number % 4 == 0, named(heavy_load, number // 4), named(common, number - number // 4 - 1))
    mixed = jax.random.permutation(jax.random.fold_in(own, 3), count)
    source_of, sink = mixed[0:count // 2 * 2:2], mixed[1:count // 2 * 2:2]
    slack = jnp.minimum(lengths[source_of] - 1, limit - lengths[sink]) // 2
    slack = jnp.where((source_of == sequence[0]) | (sink == sequence[0]) | (lengths[sink] == 0), 0, jnp.maximum(slack, 0))
    passed = jax.random.randint(jax.random.fold_in(own, 4), (count // 2,), 0, 1 << 20) % (slack + 1)
    lengths = lengths.at[source_of].add(-passed).at[sink].add(passed)
    items = jnp.searchsorted(jnp.cumsum(lengths), jnp.arange(rows * top), side="right").astype(jnp.int32)
    table = items.reshape(top, rows).T
    table = table[jax.random.permutation(jax.random.fold_in(own, 1), rows)]
    turn = jax.random.randint(jax.random.fold_in(own, 2), (rows, 1), 0, top)
    return jnp.take_along_axis(table, (jnp.arange(top)[None, :] + turn) % top, axis=1)


def load_shares(count, total, bound, slope, full):
    loads = [(1 << 20) // math.isqrt(standing ** slope) + 1 for standing in range(1, count + 1)]
    largest = bound if full else min(bound, max(-(-total // count), total * loads[0] // sum(loads)))
    least = 1 if total - largest >= count - 1 else 0
    given, surplus = [largest] + [least] * (count - 1), total - largest - least * (count - 1)
    while surplus > 0:
        candidates = [i for i in range(1, count) if given[i] < largest] or [i for i in range(1, count) if given[i] < bound]
        pool, budget = sum([loads[i] for i in candidates]), surplus
        for i in candidates:
            extra = min(bound - given[i], max(1, budget * loads[i] // pool), surplus)
            given[i] = given[i] + extra
            surplus = surplus - extra
    return np.array(given)


def gaussian(key, dims, spread, limit, pieces=(), held_as=jnp.bfloat16):
    entries = spread * jax.random.normal(key, dims, jnp.float32)
    if pieces:
        entries = entries * block_levels(key, dims, pieces, -0.22, 0.18)
    return jnp.clip(entries, -limit, limit).astype(held_as)


def setup_inputs(seed: int = 0, part: int = 0) -> dict:
    arg_keys = jax.random.split(jax.random.key(seed), 8)
    part_keys = jax.random.split(jax.random.fold_in(arg_keys[7], part), 8)
    queries = gaussian(part_keys[0], (TOKENS, D), 1.0, 6.0, ((0, 16),))
    beam_owner_keys = jax.random.split(jax.random.fold_in(part_keys[1], 1), TOKENS // TOK_DEV)
    beam_owner_turns = jax.random.permutation(jax.random.fold_in(part_keys[1], 3), TOKENS // TOK_DEV)
    beam_owner = jax.vmap(lambda own, number: shared_out(jax.random.fold_in(part_keys[1], 2), own, number, TOK_DEV, N_WIDE, KO, CAP, 2))(beam_owner_keys, beam_owner_turns).reshape((TOKENS, KO))
    beam_local = plant(jax.random.randint(part_keys[2], (TOKENS, K), 0, CL_DEV), jax.random.fold_in(part_keys[2], 1), 0, CL_DEV - 1).astype(jnp.int32)
    leaf_weight = gaussian(part_keys[3], (LEAFC, B, D), (D // 4) ** -0.5, 0.4375, ((0, 16),))
    leaf_bias = jnp.clip(jax.random.uniform(part_keys[4], (LEAFC, B), jnp.float32, -2.0, 2.0) * block_levels(part_keys[4], (LEAFC, B), ((0, 16),), -0.4, 0.0), -2.0, 2.0)
    cluster_weight = gaussian(part_keys[5], (LEAFC, D), (D // 4) ** -0.5, 0.4375, ((0, 16),))
    block_size = plant(jax.random.randint(part_keys[6], (LEAFC,), 1, B + 1), jax.random.fold_in(part_keys[6], 1), 1, B).astype(jnp.int32)
    return dict(queries=queries, beam_owner=beam_owner, beam_local=beam_local, leaf_weight=leaf_weight, leaf_bias=leaf_bias, cluster_weight=cluster_weight, block_size=block_size)


def reference(queries, beam_owner, beam_local, leaf_weight, leaf_bias, cluster_weight, block_size):
    owner_full = jnp.repeat(beam_owner, 2, axis=1)
    cluster = (owner_full * CL_DEV + beam_local).astype(jnp.int32)
    labels = jnp.arange(B, dtype=jnp.int32)

    def score_group(packed):
        query_rows, cluster_ids = packed
        query_float = query_rows.astype(jnp.float32)
        blocks = jnp.take(leaf_weight, cluster_ids, axis=0).astype(jnp.float32)
        vectors = jnp.take(cluster_weight, cluster_ids, axis=0).astype(jnp.float32)
        leaf_logit = jnp.einsum("qd,qkjd->qkj", query_float, blocks, precision=lax.Precision.HIGHEST)
        leaf_logit = leaf_logit + jnp.take(leaf_bias, cluster_ids, axis=0)
        parent = jnp.einsum("qd,qkd->qk", query_float, vectors, precision=lax.Precision.HIGHEST)
        inside = labels[None, None, :] < jnp.take(block_size, cluster_ids, axis=0)[:, :, None]
        scored = jnp.where(inside, jax.nn.sigmoid(parent)[:, :, None] * jax.nn.sigmoid(leaf_logit), 0.0)
        return scored.reshape(query_rows.shape[0], K * B)

    scored_all = lax.map(score_group, (queries.reshape(N_WIDE, TOK_DEV, D), cluster.reshape(N_WIDE, TOK_DEV, K)))
    return scored_all.reshape(TOKENS, K * B)
```

```python
import functools

import jax
import jax.numpy as jnp
from jax import lax
from jax.experimental import pallas as pl
from jax.experimental.pallas import tpu as pltpu
from jax.sharding import PartitionSpec as P

MESH = pl.DeviceIdType.MESH
NT = (((1,), (1,)), ((), ()))
QUAD = 4
SMALL = 16


def loop(count, body):
    if count <= SMALL:
        for step in range(count):
            body(step)
    else:
        lax.fori_loop(0, count, lambda step, carry: (body(step), carry)[1], 0)


def chips_along_x(devices):
    x = 1
    while 8 * x * x <= devices // 2:
        x *= 2
    return x


def kernel(
    n, nx, slots,
    q_hbm, owner_ref, local_ref, w_hbm, bias_ref, cw_hbm, size_ref,
    out_ref,
    gath, idx, w, cw, xc, stage, ret, pick,
    send_q, send_i, recv_q, recv_i, send_r, recv_r, own_sem, w_sem, cw_sem,
):
    rows, features = q_hbm.shape
    clusters = cw_hbm.shape[0]
    labels = w_hbm.shape[0] // clusters
    pair = 2 * labels
    nz = n // (2 * nx)
    quads_per_plane = nx // 2
    me = lax.axis_index("wide")
    core = lax.rem(me, 2)
    x = lax.rem(me // 2, nx)
    z = me // (2 * nx)

    def index_of(z_, x_, core_):
        return (z_ * nx + x_) * 2 + core_

    def plane(k):
        return lax.rem(z + k, nz)

    barrier = pltpu.get_barrier_semaphore()

    def greet(step):
        pl.semaphore_signal(
            barrier, inc=1, device_id={"wide": lax.rem(me + step + 1, n)}, device_id_type=MESH
        )

    loop(n - 1, greet)

    own_copy = pltpu.make_async_copy(q_hbm, gath.at[me], own_sem)
    own_copy.start()
    w_copy = pltpu.make_async_copy(w_hbm, w, w_sem)
    w_copy.start()
    cw_copy = pltpu.make_async_copy(cw_hbm, cw, cw_sem)
    cw_copy.start()

    owner = owner_ref[...]
    local = local_ref[...]
    named = jnp.concatenate(
        [owner[k // 2:k // 2 + 1] * clusters + local[k:k + 1] for k in range(local.shape[0])], axis=0
    )
    idx[me] = jnp.concatenate([named, named], axis=1)

    pl.semaphore_wait(barrier, n - 1)

    def send_chunk(source, number, slot, target):
        pltpu.make_async_remote_copy(
            src_ref=idx.at[number], dst_ref=idx.at[number],
            send_sem=send_i.at[slot], recv_sem=recv_i.at[number],
            device_id={"wide": target}, device_id_type=MESH,
        ).start()
        pltpu.make_async_remote_copy(
            src_ref=source, dst_ref=gath.at[number],
            send_sem=send_q.at[slot], recv_sem=recv_q.at[number],
            device_id={"wide": target}, device_id_type=MESH,
        ).start()

    def wait_chunk(number):
        pltpu.make_async_copy(idx.at[number], idx.at[number], recv_i.at[number]).wait()
        pltpu.make_async_copy(gath.at[number], gath.at[number], recv_q.at[number]).wait()

    def to_column(step):
        send_chunk(q_hbm, me, step, index_of(lax.rem(z + nz - 1 - step, nz), x, core))

    x_base = nz - 1
    c_base = x_base + nz * (nx - 1)

    def to_row(source, number, k):
        def one(step):
            other = lax.rem(x + 1 + step, nx)
            send_chunk(source, number, x_base + k * (nx - 1) + step, index_of(z, other, core))
        loop(nx - 1, one)

    def to_sibling(source, number, k, step):
        send_chunk(source, number, c_base + k * nx + step, index_of(z, x, 1 - core))

    to_row(q_hbm, me, 0)
    loop(nz - 1, to_column)
    to_sibling(q_hbm, me, 0, 0)

    def from_column(k):
        number = index_of(plane(k), x, core)
        wait_chunk(number)
        to_row(gath.at[number], number, k)
        to_sibling(gath.at[number], number, k, 0)

    def from_row(k):
        def one(step):
            number = index_of(plane(k), lax.rem(x + 1 + step, nx), core)
            wait_chunk(number)
            to_sibling(gath.at[number], number, k, 1 + step)
        loop(nx - 1, one)

    def from_sibling(k):
        def one(step):
            wait_chunk(index_of(plane(k), step, 1 - core))
        loop(nx, one)

    def prepare_pick():
        dev = lax.broadcasted_iota(jnp.int32, (n, rows), 0)
        hits = [owner[k:k + 1] == dev for k in range(owner.shape[0])]
        any_hit = functools.reduce(jnp.logical_or, hits)
        before = (
            lax.broadcasted_iota(jnp.int32, (rows, rows), 0)
            < lax.broadcasted_iota(jnp.int32, (rows, rows), 1)
        )
        rank = jnp.dot(
            any_hit.astype(jnp.bfloat16), before.astype(jnp.bfloat16),
            preferred_element_type=jnp.float32,
        )
        places = [
            jnp.sum(jnp.where(hit, rank, 0.0), axis=0, keepdims=True)
            + (owner[k:k + 1] * slots).astype(jnp.float32)
            for k, hit in enumerate(hits)
        ]
        place = jnp.concatenate(places + [jnp.zeros((8 - len(places), rows), jnp.float32)], axis=0)
        place = jnp.concatenate([place, jnp.zeros((8, 128 - rows), jnp.float32)], axis=1)
        place = place.T.astype(jnp.int32)
        lane = lax.broadcasted_iota(jnp.int32, (rows, n * slots), 1)
        for k in range(owner.shape[0]):
            pick[k] = (place[:rows, k:k + 1] == lane).astype(jnp.bfloat16)

    bias = bias_ref[...]
    hi = bias.astype(jnp.bfloat16)
    rest = bias - hi.astype(jnp.float32)
    mid = rest.astype(jnp.bfloat16)
    low = (rest - mid.astype(jnp.float32)).astype(jnp.bfloat16)
    size = jnp.broadcast_to(size_ref[...].astype(jnp.float32), (labels, clusters)).astype(jnp.bfloat16)
    table = jnp.concatenate([hi, mid, low, size], axis=0)

    width = QUAD * rows

    def quad_number(position):
        return plane(position // quads_per_plane) * quads_per_plane + position % quads_per_plane

    def compact(position, half, slot_of):
        first = QUAD * quad_number(position)
        lane = lax.broadcasted_iota(jnp.int32, (8, 128), 1)
        row = lax.broadcasted_iota(jnp.int32, (8, 128), 0)
        parts = []
        for p in range(QUAD // 2):
            ids = jnp.where(lane < rows, idx[first + 2 * p], idx[first + 2 * p + 1])
            ids = ids - me * clusters
            inside = (ids >= 0) & (ids < clusters)
            value = jnp.where(inside, ids, 0).astype(jnp.float32)
            even = row % 2 == 0
            c0 = jnp.sum(jnp.where(even, value, 0.0), axis=0, keepdims=True)
            c1 = jnp.sum(jnp.where(even, 0.0, value), axis=0, keepdims=True)
            hit = jnp.sum(jnp.where(even & inside, 1.0, 0.0), axis=0, keepdims=True)
            parts.append((c0, c1, hit))
        c0, c1, hit = [jnp.concatenate(v, axis=1) for v in zip(*parts)]
        qa = lax.broadcasted_iota(jnp.int32, (width, width), 0)
        qb = lax.broadcasted_iota(jnp.int32, (width, width), 1)
        before = ((qa < qb) & (qa // rows == qb // rows)).astype(jnp.bfloat16)
        rank = jnp.dot(
            jnp.broadcast_to(hit, (8, width)).astype(jnp.bfloat16), before,
            preferred_element_type=jnp.float32,
        )[:1].astype(jnp.int32)
        lane = lax.broadcasted_iota(jnp.int32, (1, width), 1)
        place = jnp.where(hit > 0.5, rank + lane // rows * slots, -1)
        taken = (
            place == lax.broadcasted_iota(jnp.int32, (QUAD * slots, width), 0)
        ).astype(jnp.bfloat16)
        row = lax.broadcasted_iota(jnp.int32, (8, width), 0)
        both = jnp.where(row == 0, c0, jnp.where(row == 1, c1, 0.0)).astype(jnp.bfloat16)
        chosen = lax.dot_general(both, taken, NT, preferred_element_type=jnp.float32)
        embedded = gath[pl.ds(first, QUAD)].reshape(width, features)
        packed = jnp.dot(taken, embedded, preferred_element_type=jnp.float32)
        xc[slot_of, half * QUAD * slots:(half + 1) * QUAD * slots] = packed.astype(jnp.bfloat16)
        return chosen[0:1], chosen[1:2]

    def score(batch, slot_of):
        chosen = [compact(2 * batch + half, half, slot_of) for half in range(2)]
        ids = [jnp.concatenate(v, axis=1).astype(jnp.int32) for v in zip(*chosen)]
        lanes = 2 * QUAD * slots
        x_rows = xc[slot_of]
        wide_ids = [jnp.broadcast_to(v, (labels, lanes)) for v in ids]
        logit = [jnp.zeros((labels, lanes), jnp.float32) for _ in ids]
        step = min(16, clusters)
        for start in range(0, clusters, step):
            block = lax.dot_general(
                w[start * labels:(start + step) * labels], x_rows, NT,
                preferred_element_type=jnp.float32,
            )
            for c in range(step):
                piece = block[c * labels:(c + 1) * labels]
                logit = [jnp.where(v == start + c, piece, a) for v, a in zip(wide_ids, logit)]
        product = lax.dot_general(cw[...], x_rows, NT, preferred_element_type=jnp.float32)
        number = lax.broadcasted_iota(jnp.int32, (clusters, lanes), 0)
        scores = []
        for v, a in zip(ids, logit):
            hot = number == v
            parent = jnp.sum(jnp.where(hot, product, 0.0), axis=0, keepdims=True)
            extra = jnp.dot(table, hot.astype(jnp.bfloat16), preferred_element_type=jnp.float32)
            b = extra[:labels] + extra[labels:2 * labels] + extra[2 * labels:3 * labels]
            used = extra[3 * labels:]
            slot = lax.broadcasted_iota(jnp.int32, (labels, lanes), 0).astype(jnp.float32)
            value = jax.nn.sigmoid(parent) * jax.nn.sigmoid(a + b)
            scores.append(jnp.where(slot < used, value, 0.0))
        scores = jnp.concatenate(scores, axis=0)
        lane = lax.broadcasted_iota(jnp.int32, (8, 128), 1)
        for half in range(2):
            first = QUAD * quad_number(2 * batch + half)
            for t in range(QUAD):
                tile = jnp.zeros((8, 128), jnp.float32)
                for g in range(QUAD):
                    part = scores[8 * g:8 * g + 8, half * 128:half * 128 + 128]
                    shift = (slots * (g - t)) % 128
                    if shift:
                        part = pltpu.roll(part, shift, axis=1)
                    tile = jnp.where(lane // slots == g, part, tile)
                stage[first + t] = tile
        for half in range(2):
            first = QUAD * quad_number(2 * batch + half)
            for t in range(QUAD):
                target = first + t

                @pl.when(target != me)
                def _():
                    pltpu.make_async_remote_copy(
                        src_ref=stage.at[target], dst_ref=ret.at[me],
                        send_sem=send_r.at[target], recv_sem=recv_r.at[me],
                        device_id={"wide": target}, device_id_type=MESH,
                    ).start()

                @pl.when(target == me)
                def _():
                    ret[me] = stage[me]

    batches = n // (2 * QUAD)
    if n <= SMALL and nx == 2:
        own_copy.wait()
        for k in range(1, nz):
            from_column(k)
            from_row(k - 1)
            if k == 1:
                prepare_pick()
                w_copy.wait()
                cw_copy.wait()
        from_sibling(0)
        from_sibling(1)
        score(0, 0)
        from_row(nz - 1)
        from_sibling(2)
        from_sibling(3)
        score(1, 1)
    else:
        prepare_pick()
        own_copy.wait()
        from_row(0)

        def relay(step):
            from_column(step + 1)
            from_row(step + 1)

        loop(nz - 1, relay)
        loop(nz, from_sibling)
        w_copy.wait()
        cw_copy.wait()
        lax.fori_loop(0, batches, lambda b, carry: (score(b, 0), carry)[1], 0)

    def wait_return(step):
        source = lax.rem(me + 1 + step, n)
        pltpu.make_async_copy(ret.at[source], ret.at[source], recv_r.at[source]).wait()

    loop(n - 1, wait_return)

    lane = lax.broadcasted_iota(jnp.int32, (8, 128), 1)
    columns = []
    for d in range(0, n, QUAD):
        tiles = [ret[d + t] for t in range(QUAD)]
        parts = []
        for g in range(QUAD):
            part = jnp.zeros((8, 128), jnp.float32)
            for t in range(QUAD):
                shift = (slots * (t - g)) % 128
                moved = pltpu.roll(tiles[t], shift, axis=1) if shift else tiles[t]
                part = jnp.where(lane // slots == t, moved, part)
            parts.append(part)
        columns.append(jnp.concatenate(parts, axis=0))
    back = jnp.concatenate(columns, axis=1)
    head = back.astype(jnp.bfloat16)
    tail = (back - head.astype(jnp.float32)).astype(jnp.bfloat16)
    result = jnp.zeros(out_ref.shape, jnp.float32)
    owners = owner.shape[0]
    for term in (head, tail):
        for k in range(owners):
            spread = jnp.concatenate(
                [term if j == k else jnp.zeros_like(term) for j in range(owners)], axis=0
            )
            result += lax.dot_general(pick[k], spread, NT, preferred_element_type=jnp.float32)
    out_ref[...] = result

    def wait_sent(step):
        pltpu.make_async_copy(idx.at[0], idx.at[0], send_i.at[step]).wait()
        pltpu.make_async_copy(gath.at[0], gath.at[0], send_q.at[step]).wait()

    def wait_returned(step):
        target = lax.rem(me + 1 + step, n)
        pltpu.make_async_copy(stage.at[target], stage.at[target], send_r.at[target]).wait()

    loop(n - 1, wait_sent)
    loop(n - 1, wait_returned)


def on_device(n, queries, beam_owner, beam_local, leaf_weight, leaf_bias, cluster_weight, block_size):
    rows, features = queries.shape
    owners = beam_owner.shape[1]
    clusters, labels, _ = leaf_weight.shape
    slots = max(32, 2 * rows * owners // n)
    assert slots == 32 and rows == 64 and 2 * labels * owners == 128 and n % 8 == 0
    vmem = pl.BlockSpec(memory_space=pltpu.VMEM)
    hbm = pl.BlockSpec(memory_space=pl.ANY)
    dma = pltpu.SemaphoreType.DMA
    return pl.pallas_call(
        functools.partial(kernel, n, chips_along_x(n), slots),
        out_shape=jax.ShapeDtypeStruct((rows, 2 * labels * owners), jnp.float32),
        in_specs=[hbm, vmem, vmem, hbm, vmem, hbm, vmem],
        out_specs=vmem,
        scratch_shapes=[
            pltpu.VMEM((n, rows, features), queries.dtype),
            pltpu.VMEM((n, 8, 128), jnp.int32),
            pltpu.VMEM((clusters * labels, features), leaf_weight.dtype),
            pltpu.VMEM((clusters, features), cluster_weight.dtype),
            pltpu.VMEM((2, 2 * QUAD * slots, features), jnp.bfloat16),
            pltpu.VMEM((n, 8, 128), jnp.float32),
            pltpu.VMEM((n, 8, 128), jnp.float32),
            pltpu.VMEM((owners, rows, n * slots), jnp.bfloat16),
            dma((n - 1,)), dma((n - 1,)), dma((n,)), dma((n,)), dma((n,)), dma((n,)),
            dma, dma, dma,
        ],
        compiler_params=pltpu.CompilerParams(
            collective_id=0, has_side_effects=True, vmem_limit_bytes=48 * 2**20
        ),
    )(
        queries,
        beam_owner.T,
        beam_local.T,
        leaf_weight.reshape(clusters * labels, features),
        leaf_bias.T,
        cluster_weight,
        block_size.reshape(1, clusters),
    )


def solution(mesh):
    spec = P(("groups", "wide"))
    return jax.shard_map(
        functools.partial(on_device, mesh.shape["wide"]),
        mesh=mesh,
        in_specs=(spec,) * 7,
        out_specs=spec,
        check_vma=False,
    )
```

```python
import functools

import jax
import jax.numpy as jnp
from jax import lax
from jax.experimental import pallas as pl
from jax.experimental.pallas import tpu as pltpu
from jax.sharding import PartitionSpec as P

MESH = pl.DeviceIdType.MESH
NT = (((1,), (1,)), ((), ()))
QUAD = 4
SMALL = 16


def loop(count, body):
    if count <= SMALL:
        for step in range(count):
            body(step)
    else:
        lax.fori_loop(0, count, lambda step, carry: (body(step), carry)[1], 0)


def chips_along_x(devices):
    x = 1
    while 8 * x * x <= devices // 2:
        x *= 2
    return x


def kernel(
    n, nx, slots,
    q_hbm, owner_hbm, local_hbm, w_hbm, bias_hbm, cw_hbm, size_hbm,
    out_ref,
    gath, idx, w, cw, xc, stage, ret, pick, owner_ref, local_ref, bias_ref, size_ref, table,
    send_q, send_i, recv_q, recv_i, send_r, recv_r, load_sem,
):
    rows, features = q_hbm.shape
    clusters = cw_hbm.shape[0]
    labels = w_hbm.shape[0] // clusters
    pair = 2 * labels
    nz = n // (2 * nx)
    quads_per_plane = nx // 2
    me = lax.axis_index("wide")
    core = lax.rem(me, 2)
    x = lax.rem(me // 2, nx)
    z = me // (2 * nx)

    def index_of(z_, x_, core_):
        return (z_ * nx + x_) * 2 + core_

    def plane(k):
        return lax.rem(z + k, nz)

    barrier = pltpu.get_barrier_semaphore()

    def greet(step):
        pl.semaphore_signal(
            barrier, inc=1, device_id={"wide": lax.rem(me + step + 1, n)}, device_id_type=MESH
        )

    loop(n - 1, greet)

    loads = [
        pltpu.make_async_copy(source, target, load_sem.at[i])
        for i, (source, target) in enumerate([
            (owner_hbm, owner_ref), (local_hbm, local_ref), (q_hbm, gath.at[me]),
            (size_hbm, size_ref), (bias_hbm, bias_ref), (cw_hbm, cw), (w_hbm, w),
        ])
    ]
    for load in loads:
        load.start()
    owner_copy, local_copy, own_copy, size_copy, bias_copy, cw_copy, w_copy = loads
    owner_copy.wait()
    local_copy.wait()

    owner = owner_ref[...]
    local = local_ref[...]
    named = jnp.concatenate(
        [owner[k // 2:k // 2 + 1] * clusters + local[k:k + 1] for k in range(local.shape[0])], axis=0
    )
    idx[me] = jnp.concatenate([named, named], axis=1)

    pl.semaphore_wait(barrier, n - 1)

    def send_chunk(source, number, slot, target):
        pltpu.make_async_remote_copy(
            src_ref=idx.at[number], dst_ref=idx.at[number],
            send_sem=send_i.at[slot], recv_sem=recv_i.at[number],
            device_id={"wide": target}, device_id_type=MESH,
        ).start()
        pltpu.make_async_remote_copy(
            src_ref=source, dst_ref=gath.at[number],
            send_sem=send_q.at[slot], recv_sem=recv_q.at[number],
            device_id={"wide": target}, device_id_type=MESH,
        ).start()

    def wait_chunk(number):
        pltpu.make_async_copy(idx.at[number], idx.at[number], recv_i.at[number]).wait()
        pltpu.make_async_copy(gath.at[number], gath.at[number], recv_q.at[number]).wait()

    def to_column(step):
        send_chunk(q_hbm, me, step, index_of(lax.rem(z + nz - 1 - step, nz), x, core))

    x_base = nz - 1
    c_base = x_base + nz * (nx - 1)

    def to_row(source, number, k):
        def one(step):
            other = lax.rem(x + 1 + step, nx)
            send_chunk(source, number, x_base + k * (nx - 1) + step, index_of(z, other, core))
        loop(nx - 1, one)

    def to_sibling(source, number, k, step):
        send_chunk(source, number, c_base + k * nx + step, index_of(z, x, 1 - core))

    to_row(q_hbm, me, 0)
    loop(nz - 1, to_column)
    to_sibling(q_hbm, me, 0, 0)

    def from_column(k):
        number = index_of(plane(k), x, core)
        wait_chunk(number)
        to_row(gath.at[number], number, k)
        to_sibling(gath.at[number], number, k, 0)

    def from_row(k):
        def one(step):
            number = index_of(plane(k), lax.rem(x + 1 + step, nx), core)
            wait_chunk(number)
            to_sibling(gath.at[number], number, k, 1 + step)
        loop(nx - 1, one)

    def from_sibling(k):
        def one(step):
            wait_chunk(index_of(plane(k), step, 1 - core))
        loop(nx, one)

    def make_table():
        size_copy.wait()
        bias_copy.wait()
        bias = bias_ref[...]
        hi = bias.astype(jnp.bfloat16)
        rest = bias - hi.astype(jnp.float32)
        mid = rest.astype(jnp.bfloat16)
        low = (rest - mid.astype(jnp.float32)).astype(jnp.bfloat16)
        size = jnp.broadcast_to(size_ref[...].astype(jnp.float32), (labels, clusters))
        table[...] = jnp.concatenate([hi, mid, low, size.astype(jnp.bfloat16)], axis=0)

    def prepare_pick():
        dev = lax.broadcasted_iota(jnp.int32, (n, rows), 0)
        hits = [owner[k:k + 1] == dev for k in range(owner.shape[0])]
        any_hit = functools.reduce(jnp.logical_or, hits)
        before = (
            lax.broadcasted_iota(jnp.int32, (rows, rows), 0)
            < lax.broadcasted_iota(jnp.int32, (rows, rows), 1)
        )
        rank = jnp.dot(
            any_hit.astype(jnp.bfloat16), before.astype(jnp.bfloat16),
            preferred_element_type=jnp.float32,
        )
        places = [
            jnp.sum(jnp.where(hit, rank, 0.0), axis=0, keepdims=True)
            + (owner[k:k + 1] * slots).astype(jnp.float32)
            for k, hit in enumerate(hits)
        ]
        place = jnp.concatenate(places + [jnp.zeros((8 - len(places), rows), jnp.float32)], axis=0)
        place = jnp.concatenate([place, jnp.zeros((8, 128 - rows), jnp.float32)], axis=1)
        place = place.T.astype(jnp.int32)
        lane = lax.broadcasted_iota(jnp.int32, (rows, n * slots), 1)
        for k in range(owner.shape[0]):
            pick[k] = (place[:rows, k:k + 1] == lane).astype(jnp.bfloat16)

    width = QUAD * rows

    def quad_number(position):
        return plane(position // quads_per_plane) * quads_per_plane + position % quads_per_plane

    def compact(position, half, slot_of):
        first = QUAD * quad_number(position)
        lane = lax.broadcasted_iota(jnp.int32, (8, 128), 1)
        row = lax.broadcasted_iota(jnp.int32, (8, 128), 0)
        parts = []
        for p in range(QUAD // 2):
            ids = jnp.where(lane < rows, idx[first + 2 * p], idx[first + 2 * p + 1])
            ids = ids - me * clusters
            inside = (ids >= 0) & (ids < clusters)
            value = jnp.where(inside, ids, 0).astype(jnp.float32)
            even = row % 2 == 0
            c0 = jnp.sum(jnp.where(even, value, 0.0), axis=0, keepdims=True)
            c1 = jnp.sum(jnp.where(even, 0.0, value), axis=0, keepdims=True)
            hit = jnp.sum(jnp.where(even & inside, 1.0, 0.0), axis=0, keepdims=True)
            parts.append((c0, c1, hit))
        c0, c1, hit = [jnp.concatenate(v, axis=1) for v in zip(*parts)]
        qa = lax.broadcasted_iota(jnp.int32, (width, width), 0)
        qb = lax.broadcasted_iota(jnp.int32, (width, width), 1)
        before = ((qa < qb) & (qa // rows == qb // rows)).astype(jnp.bfloat16)
        rank = jnp.dot(
            jnp.broadcast_to(hit, (8, width)).astype(jnp.bfloat16), before,
            preferred_element_type=jnp.float32,
        )[:1].astype(jnp.int32)
        lane = lax.broadcasted_iota(jnp.int32, (1, width), 1)
        place = jnp.where(hit > 0.5, rank + lane // rows * slots, -1)
        taken = (
            place == lax.broadcasted_iota(jnp.int32, (QUAD * slots, width), 0)
        ).astype(jnp.bfloat16)
        row = lax.broadcasted_iota(jnp.int32, (8, width), 0)
        both = jnp.where(row == 0, c0, jnp.where(row == 1, c1, 0.0)).astype(jnp.bfloat16)
        chosen = lax.dot_general(both, taken, NT, preferred_element_type=jnp.float32)
        embedded = gath[pl.ds(first, QUAD)].reshape(width, features)
        packed = jnp.dot(taken, embedded, preferred_element_type=jnp.float32)
        xc[slot_of, half * QUAD * slots:(half + 1) * QUAD * slots] = packed.astype(jnp.bfloat16)
        return chosen[0:1], chosen[1:2]

    def score(batch, slot_of):
        chosen = [compact(2 * batch + half, half, slot_of) for half in range(2)]
        ids = [jnp.concatenate(v, axis=1).astype(jnp.int32) for v in zip(*chosen)]
        lanes = 2 * QUAD * slots
        x_rows = xc[slot_of]
        wide_ids = [jnp.broadcast_to(v, (labels, lanes)) for v in ids]
        logit = [jnp.zeros((labels, lanes), jnp.float32) for _ in ids]
        step = min(16, clusters)
        for start in range(0, clusters, step):
            block = lax.dot_general(
                w[start * labels:(start + step) * labels], x_rows, NT,
                preferred_element_type=jnp.float32,
            )
            for c in range(step):
                piece = block[c * labels:(c + 1) * labels]
                logit = [jnp.where(v == start + c, piece, a) for v, a in zip(wide_ids, logit)]
        product = lax.dot_general(cw[...], x_rows, NT, preferred_element_type=jnp.float32)
        number = lax.broadcasted_iota(jnp.int32, (clusters, lanes), 0)
        scores = []
        for v, a in zip(ids, logit):
            hot = number == v
            parent = jnp.sum(jnp.where(hot, product, 0.0), axis=0, keepdims=True)
            extra = jnp.dot(table[...], hot.astype(jnp.bfloat16), preferred_element_type=jnp.float32)
            b = extra[:labels] + extra[labels:2 * labels] + extra[2 * labels:3 * labels]
            used = extra[3 * labels:]
            slot = lax.broadcasted_iota(jnp.int32, (labels, lanes), 0).astype(jnp.float32)
            value = jax.nn.sigmoid(parent) * jax.nn.sigmoid(a + b)
            scores.append(jnp.where(slot < used, value, 0.0))
        scores = jnp.concatenate(scores, axis=0)
        lane = lax.broadcasted_iota(jnp.int32, (8, 128), 1)
        for half in range(2):
            first = QUAD * quad_number(2 * batch + half)
            for t in range(QUAD):
                tile = jnp.zeros((8, 128), jnp.float32)
                for g in range(QUAD):
                    part = scores[8 * g:8 * g + 8, half * 128:half * 128 + 128]
                    shift = (slots * (g - t)) % 128
                    if shift:
                        part = pltpu.roll(part, shift, axis=1)
                    tile = jnp.where(lane // slots == g, part, tile)
                stage[first + t] = tile
        for half in range(2):
            first = QUAD * quad_number(2 * batch + half)
            for t in range(QUAD):
                target = first + t

                @pl.when(target != me)
                def _():
                    pltpu.make_async_remote_copy(
                        src_ref=stage.at[target], dst_ref=ret.at[me],
                        send_sem=send_r.at[target], recv_sem=recv_r.at[me],
                        device_id={"wide": target}, device_id_type=MESH,
                    ).start()

                @pl.when(target == me)
                def _():
                    ret[me] = stage[me]

    batches = n // (2 * QUAD)
    if n <= SMALL and nx == 2:
        own_copy.wait()
        for k in range(1, nz):
            from_column(k)
            from_row(k - 1)
            if k == 1:
                prepare_pick()
                make_table()
                w_copy.wait()
                cw_copy.wait()
        from_sibling(0)
        from_sibling(1)
        score(0, 0)
        from_row(nz - 1)
        from_sibling(2)
        from_sibling(3)
        score(1, 1)
    else:
        prepare_pick()
        make_table()
        own_copy.wait()
        from_row(0)

        def relay(step):
            from_column(step + 1)
            from_row(step + 1)

        loop(nz - 1, relay)
        loop(nz, from_sibling)
        w_copy.wait()
        cw_copy.wait()
        lax.fori_loop(0, batches, lambda b, carry: (score(b, 0), carry)[1], 0)

    def wait_return(step):
        source = lax.rem(me + 1 + step, n)
        pltpu.make_async_copy(ret.at[source], ret.at[source], recv_r.at[source]).wait()

    loop(n - 1, wait_return)

    lane = lax.broadcasted_iota(jnp.int32, (8, 128), 1)
    columns = []
    for d in range(0, n, QUAD):
        tiles = [ret[d + t] for t in range(QUAD)]
        parts = []
        for g in range(QUAD):
            part = jnp.zeros((8, 128), jnp.float32)
            for t in range(QUAD):
                shift = (slots * (t - g)) % 128
                moved = pltpu.roll(tiles[t], shift, axis=1) if shift else tiles[t]
                part = jnp.where(lane // slots == t, moved, part)
            parts.append(part)
        columns.append(jnp.concatenate(parts, axis=0))
    back = jnp.concatenate(columns, axis=1)
    head = back.astype(jnp.bfloat16)
    tail = (back - head.astype(jnp.float32)).astype(jnp.bfloat16)
    result = jnp.zeros(out_ref.shape, jnp.float32)
    owners = owner.shape[0]
    for term in (head, tail):
        for k in range(owners):
            spread = jnp.concatenate(
                [term if j == k else jnp.zeros_like(term) for j in range(owners)], axis=0
            )
            result += lax.dot_general(pick[k], spread, NT, preferred_element_type=jnp.float32)
    out_ref[...] = result

    def wait_sent(step):
        pltpu.make_async_copy(idx.at[0], idx.at[0], send_i.at[step]).wait()
        pltpu.make_async_copy(gath.at[0], gath.at[0], send_q.at[step]).wait()

    def wait_returned(step):
        target = lax.rem(me + 1 + step, n)
        pltpu.make_async_copy(stage.at[target], stage.at[target], send_r.at[target]).wait()

    loop(n - 1, wait_sent)
    loop(n - 1, wait_returned)


def on_device(n, queries, beam_owner, beam_local, leaf_weight, leaf_bias, cluster_weight, block_size):
    rows, features = queries.shape
    owners = beam_owner.shape[1]
    clusters, labels, _ = leaf_weight.shape
    slots = max(32, 2 * rows * owners // n)
    assert slots == 32 and rows == 64 and 2 * labels * owners == 128 and n % 8 == 0
    vmem = pl.BlockSpec(memory_space=pltpu.VMEM)
    hbm = pl.BlockSpec(memory_space=pltpu.HBM)
    dma = pltpu.SemaphoreType.DMA
    return pl.pallas_call(
        functools.partial(kernel, n, chips_along_x(n), slots),
        out_shape=jax.ShapeDtypeStruct((rows, 2 * labels * owners), jnp.float32),
        in_specs=[hbm] * 7,
        out_specs=vmem,
        scratch_shapes=[
            pltpu.VMEM((n, rows, features), queries.dtype),
            pltpu.VMEM((n, 8, 128), jnp.int32),
            pltpu.VMEM((clusters * labels, features), leaf_weight.dtype),
            pltpu.VMEM((clusters, features), cluster_weight.dtype),
            pltpu.VMEM((2, 2 * QUAD * slots, features), jnp.bfloat16),
            pltpu.VMEM((n, 8, 128), jnp.float32),
            pltpu.VMEM((n, 8, 128), jnp.float32),
            pltpu.VMEM((owners, rows, n * slots), jnp.bfloat16),
            pltpu.VMEM((owners, rows), jnp.int32),
            pltpu.VMEM((2 * owners, rows), jnp.int32),
            pltpu.VMEM((labels, clusters), jnp.float32),
            pltpu.VMEM((1, clusters), jnp.int32),
            pltpu.VMEM((4 * labels, clusters), jnp.bfloat16),
            dma((n - 1,)), dma((n - 1,)), dma((n,)), dma((n,)), dma((n,)), dma((n,)),
            dma((7,)),
        ],
        compiler_params=pltpu.CompilerParams(
            collective_id=0, has_side_effects=True, vmem_limit_bytes=56 * 2**20
        ),
    )(
        queries,
        beam_owner.T,
        beam_local.T,
        leaf_weight.reshape(clusters * labels, features),
        leaf_bias.T,
        cluster_weight,
        block_size.reshape(1, clusters),
    )


def solution(mesh):
    spec = P(("groups", "wide"))
    return jax.shard_map(
        functools.partial(on_device, mesh.shape["wide"]),
        mesh=mesh,
        in_specs=(spec,) * 7,
        out_specs=spec,
        check_vma=False,
    )
```

```python
import functools

import jax
import jax.numpy as jnp
from jax import lax
from jax.experimental import pallas as pl
from jax.experimental.pallas import tpu as pltpu
from jax.sharding import PartitionSpec as P

MESH = pl.DeviceIdType.MESH
NT = (((1,), (1,)), ((), ()))
QUAD = 4
SMALL = 16


def loop(count, body):
    if count <= SMALL:
        for step in range(count):
            body(step)
    else:
        lax.fori_loop(0, count, lambda step, carry: (body(step), carry)[1], 0)


def chips_along_x(devices):
    x = 1
    while 8 * x * x <= devices // 2:
        x *= 2
    return x


def kernel(
    n, nx, slots, pieces,
    q_hbm, owner_hbm, local_hbm, w_hbm, bias_hbm, cw_hbm, size_hbm,
    out_ref,
    gath, idx, w, cw, xc, stage, ret, pick, owner_ref, local_ref, bias_ref, size_ref, table,
    send_q, send_i, recv_i, send_r, recv_r, recv_z, recv_x, recv_c, recv_zi, recv_xi, load_sem,
):
    rows, features = q_hbm.shape
    clusters = cw_hbm.shape[0]
    labels = w_hbm.shape[0] // clusters
    pair = 2 * labels
    nz = n // (2 * nx)
    quads_per_plane = nx // 2
    piece = rows // pieces
    me = lax.axis_index("wide")
    core = lax.rem(me, 2)
    x = lax.rem(me // 2, nx)
    z = me // (2 * nx)

    def index_of(z_, x_, core_):
        return (z_ * nx + x_) * 2 + core_

    def plane(k):
        other, bit = 0, 1
        while bit < nz:
            mine, turned = lax.rem(z // bit, 2), k // bit % 2
            other = other + bit * (mine + turned - 2 * mine * turned)
            bit *= 2
        return other

    barrier = pltpu.get_barrier_semaphore()

    def greet(target):
        pl.semaphore_signal(barrier, inc=1, device_id={"wide": target}, device_id_type=MESH)

    loop(nz - 1, lambda step: greet(index_of(plane(step + 1), x, core)))
    loop(nx - 1, lambda step: greet(index_of(z, lax.rem(x + 1 + step, nx), core)))
    greet(index_of(z, x, 1 - core))

    loads = [
        pltpu.make_async_copy(source, target, load_sem.at[i])
        for i, (source, target) in enumerate([
            (owner_hbm, owner_ref), (local_hbm, local_ref), (q_hbm, gath.at[me]),
            (size_hbm, size_ref), (bias_hbm, bias_ref), (cw_hbm, cw), (w_hbm, w),
        ])
    ]
    for load in loads:
        load.start()
    owner_copy, local_copy, own_copy, size_copy, bias_copy, cw_copy, w_copy = loads
    owner_copy.wait()
    local_copy.wait()

    owner = owner_ref[...]
    local = local_ref[...]
    named = jnp.concatenate(
        [owner[k // 2:k // 2 + 1] * clusters + local[k:k + 1] for k in range(local.shape[0])], axis=0
    )
    half_beams = local.shape[0] // 2
    idx[me] = jnp.concatenate([named[:half_beams], named[half_beams:]], axis=1)

    own_copy.wait()
    pl.semaphore_wait(barrier, nz + nx - 1)

    def send_idx(number, recv, target):
        pltpu.make_async_remote_copy(
            src_ref=idx.at[number], dst_ref=idx.at[number], send_sem=send_i, recv_sem=recv,
            device_id={"wide": target}, device_id_type=MESH,
        ).start()

    def wait_one(ref, sem):
        pltpu.make_async_copy(ref, ref, sem).wait()

    def part(number, p):
        return gath.at[number, pl.ds(p * piece, piece)]

    def send(source, number, p, recv, target):
        pltpu.make_async_remote_copy(
            src_ref=source, dst_ref=part(number, p), send_sem=send_q, recv_sem=recv,
            device_id={"wide": target}, device_id_type=MESH,
        ).start()

    def to_column(k, p):
        if p == 0:
            send_idx(me, recv_zi.at[k], index_of(plane(k), x, core))
        send(own_part(p), me, p, recv_z.at[k * pieces + p], index_of(plane(k), x, core))

    def to_row(source, number, k, p):
        def one(step):
            other = lax.rem(x + 1 + step, nx)
            if p == 0:
                send_idx(number, recv_xi.at[k * (nx - 1) + step], index_of(z, other, core))
            send(source, number, p, recv_x.at[(k * (nx - 1) + step) * pieces + p], index_of(z, other, core))
        loop(nx - 1, one)

    def to_sibling(source, number, k, p):
        if p == 0:
            send_idx(number, recv_i.at[k], index_of(z, x, 1 - core))
        send(source, number, p, recv_c.at[k], index_of(z, x, 1 - core))

    def own_part(p):
        return part(me, p)

    def from_column(k, pass_on=False):
        number = index_of(plane(k), x, core)
        wait_one(idx.at[number], recv_zi.at[k])
        for p in range(pieces):
            pltpu.make_async_copy(part(number, p), part(number, p), recv_z.at[k * pieces + p]).wait()
            to_row(part(number, p), number, k, p)
            if pass_on:
                @pl.when(middle)
                def _():
                    if p == 0:
                        send_idx(number, recv_zi.at[2], index_of(plane(1), x, core))
                    send(part(number, p), number, p, recv_z.at[2 * pieces + p], index_of(plane(1), x, core))
            to_sibling(part(number, p), number, k, p)

    def from_row(k):
        def one(step):
            number = index_of(plane(k), lax.rem(x + nx - 1 - step, nx), core)
            wait_one(idx.at[number], recv_xi.at[k * (nx - 1) + step])
            for p in range(pieces):
                recv = recv_x.at[(k * (nx - 1) + step) * pieces + p]
                pltpu.make_async_copy(part(number, p), part(number, p), recv).wait()
                to_sibling(part(number, p), number, k, p)
        loop(nx - 1, one)

    def from_sibling(k):
        some = gath.at[pl.ds(0, nx)]
        pltpu.make_async_copy(some, some, recv_c.at[k]).wait()

    relayed = n <= SMALL and nx == 2 and nz == 4
    middle = (z == 1) | (z == 2)

    def relay_order(step):
        return jnp.where(middle, (3, 1, 2)[step], step + 1)

    order = [0] + [relay_order(step) for step in range(3)]

    if not relayed:
        for p in range(pieces):
            to_row(own_part(p), me, 0, p)
    if relayed:
        for p in range(pieces):
            to_column(1, p)
            to_row(own_part(p), me, 0, p)

            @pl.when(middle)
            def _():
                to_column(3, p)

        @pl.when(jnp.logical_not(middle))
        def _():
            for k in (2, 3):
                for p in range(pieces):
                    to_column(k, p)
    else:
        loop(nz - 1, lambda step: [to_column(step + 1, p) for p in range(pieces)])
    for p in range(pieces):
        to_sibling(own_part(p), me, 0, p)

    def make_table():
        size_copy.wait()
        bias_copy.wait()
        bias = bias_ref[...]
        hi = bias.astype(jnp.bfloat16)
        rest = bias - hi.astype(jnp.float32)
        mid = rest.astype(jnp.bfloat16)
        low = (rest - mid.astype(jnp.float32)).astype(jnp.bfloat16)
        size = jnp.broadcast_to(size_ref[...].astype(jnp.float32), (labels, clusters))
        table[...] = jnp.concatenate([hi, mid, low, size.astype(jnp.bfloat16)], axis=0)

    def prepare_pick():
        dev = lax.broadcasted_iota(jnp.int32, (n, rows), 0)
        hits = [owner[k:k + 1] == dev for k in range(owner.shape[0])]
        any_hit = functools.reduce(jnp.logical_or, hits)
        before = (
            lax.broadcasted_iota(jnp.int32, (rows, rows), 0)
            < lax.broadcasted_iota(jnp.int32, (rows, rows), 1)
        )
        rank = jnp.dot(
            any_hit.astype(jnp.bfloat16), before.astype(jnp.bfloat16),
            preferred_element_type=jnp.float32,
        )
        places = [
            jnp.sum(jnp.where(hit, rank, 0.0), axis=0, keepdims=True)
            + (owner[k:k + 1] * slots).astype(jnp.float32)
            for k, hit in enumerate(hits)
        ]
        place = jnp.concatenate(places + [jnp.zeros((8 - len(places), rows), jnp.float32)], axis=0)
        place = jnp.concatenate([place, jnp.zeros((8, 128 - rows), jnp.float32)], axis=1)
        place = place.T.astype(jnp.int32)
        lane = lax.broadcasted_iota(jnp.int32, (rows, n * slots), 1)
        for k in range(owner.shape[0]):
            pick[k] = (place[:rows, k:k + 1] == lane).astype(jnp.bfloat16)

    width = QUAD * rows

    def quad_number(position):
        if relayed:
            return plane(order[position])
        return plane(position // quads_per_plane) * quads_per_plane + position % quads_per_plane

    def choose(position):
        first = QUAD * quad_number(position)
        lane = lax.broadcasted_iota(jnp.int32, (half_beams, 128), 1)
        row = lax.broadcasted_iota(jnp.int32, (2 * half_beams, 128), 0)
        parts = []
        for p in range(QUAD // 2):
            left, right = idx[first + 2 * p], idx[first + 2 * p + 1]
            ids = jnp.concatenate([
                jnp.where(lane < rows, left, pltpu.roll(right, rows, axis=1)),
                jnp.where(lane < rows, pltpu.roll(left, rows, axis=1), right),
            ], axis=0)
            ids = ids - me * clusters
            inside = (ids >= 0) & (ids < clusters)
            value = jnp.where(inside, ids, 0).astype(jnp.float32)
            even = lax.rem(row, 2) == 0
            c0 = jnp.sum(jnp.where(even, value, 0.0), axis=0, keepdims=True)
            c1 = jnp.sum(jnp.where(even, 0.0, value), axis=0, keepdims=True)
            hit = jnp.sum(jnp.where(even & inside, 1.0, 0.0), axis=0, keepdims=True)
            parts.append((c0, c1, hit))
        c0, c1, hit = [jnp.concatenate(v, axis=1) for v in zip(*parts)]
        qa = lax.broadcasted_iota(jnp.int32, (width, width), 0)
        qb = lax.broadcasted_iota(jnp.int32, (width, width), 1)
        before = ((qa < qb) & (qa // rows == qb // rows)).astype(jnp.bfloat16)
        rank = jnp.dot(
            jnp.broadcast_to(hit, (8, width)).astype(jnp.bfloat16), before,
            preferred_element_type=jnp.float32,
        )[:1].astype(jnp.int32)
        lane = lax.broadcasted_iota(jnp.int32, (1, width), 1)
        place = jnp.where(hit > 0.5, rank + lane // rows * slots, -1)
        taken = (
            place == lax.broadcasted_iota(jnp.int32, (QUAD * slots, width), 0)
        ).astype(jnp.bfloat16)
        row = lax.broadcasted_iota(jnp.int32, (8, width), 0)
        both = jnp.where(row == 0, c0, jnp.where(row == 1, c1, 0.0)).astype(jnp.bfloat16)
        chosen = lax.dot_general(both, taken, NT, preferred_element_type=jnp.float32)
        return first, taken, chosen[0:1], chosen[1:2]

    def score(picks, slot_of):
        lanes = QUAD * slots * len(picks)
        for place, (first, taken, _, _) in enumerate(picks):
            embedded = gath[pl.ds(first, QUAD)].reshape(width, features)
            packed = jnp.dot(taken, embedded, preferred_element_type=jnp.float32)
            xc[slot_of, place * QUAD * slots:(place + 1) * QUAD * slots] = packed.astype(jnp.bfloat16)
        ids = [jnp.concatenate([v[2 + k] for v in picks], axis=1).astype(jnp.int32) for k in range(2)]
        x_rows = xc[slot_of, :lanes]
        wide_ids = [jnp.broadcast_to(v, (labels, lanes)) for v in ids]
        logit = [jnp.zeros((labels, lanes), jnp.float32) for _ in ids]
        step = min(16, clusters)
        for start in range(0, clusters, step):
            block = lax.dot_general(
                w[start * labels:(start + step) * labels], x_rows, NT,
                preferred_element_type=jnp.float32,
            )
            for c in range(step):
                piece = block[c * labels:(c + 1) * labels]
                logit = [jnp.where(v == start + c, piece, a) for v, a in zip(wide_ids, logit)]
        product = lax.dot_general(cw[...], x_rows, NT, preferred_element_type=jnp.float32)
        number = lax.broadcasted_iota(jnp.int32, (clusters, lanes), 0)
        scores = []
        for v, a in zip(ids, logit):
            hot = number == v
            parent = jnp.sum(jnp.where(hot, product, 0.0), axis=0, keepdims=True)
            extra = jnp.dot(table[...], hot.astype(jnp.bfloat16), preferred_element_type=jnp.float32)
            b = extra[:labels] + extra[labels:2 * labels] + extra[2 * labels:3 * labels]
            used = extra[3 * labels:]
            slot = lax.broadcasted_iota(jnp.int32, (labels, lanes), 0).astype(jnp.float32)
            value = jax.nn.sigmoid(parent) * jax.nn.sigmoid(a + b)
            scores.append(jnp.where(slot < used, value, 0.0))
        scores = jnp.concatenate(scores, axis=0)
        lane = lax.broadcasted_iota(jnp.int32, (8, 128), 1)
        for half, (first, _, _, _) in enumerate(picks):
            for t in range(QUAD):
                tile = jnp.zeros((8, 128), jnp.float32)
                for g in range(QUAD):
                    part = scores[8 * g:8 * g + 8, half * 128:half * 128 + 128]
                    shift = (slots * (g - t)) % 128
                    if shift:
                        part = pltpu.roll(part, shift, axis=1)
                    tile = jnp.where(lane // slots == g, part, tile)
                stage[first + t] = tile
        for first, _, _, _ in picks:
            for t in range(QUAD):
                target = first + t

                @pl.when(target != me)
                def _():
                    pltpu.make_async_remote_copy(
                        src_ref=stage.at[target], dst_ref=ret.at[me],
                        send_sem=send_r, recv_sem=recv_r,
                        device_id={"wide": target}, device_id_type=MESH,
                    ).start()

                @pl.when(target == me)
                def _():
                    ret[me] = stage[me]

    batches = n // (2 * QUAD)

    def wait_idx(k):
        wait_one(idx.at[pl.ds(0, nx)], recv_i.at[k])

    prepare_pick()
    make_table()
    if relayed:
        from_column(order[1], pass_on=True)
        from_row(order[0])
        from_column(order[2])
        from_row(order[1])
        from_column(order[3])
        from_row(order[2])
        from_sibling(order[0])
        from_sibling(order[1])
        w_copy.wait()
        cw_copy.wait()
        wait_idx(order[0])
        wait_idx(order[1])
        score([choose(0), choose(1)], 0)
        wait_idx(order[2])
        picks = [choose(2)]
        from_row(order[3])
        wait_idx(order[3])
        picks.append(choose(3))
        from_sibling(order[2])
        from_sibling(order[3])
        score(picks, 1)
    else:
        from_row(0)

        def relay(step):
            from_column(step + 1)
            from_row(step + 1)

        loop(nz - 1, relay)
        loop(nz, from_sibling)
        w_copy.wait()
        cw_copy.wait()
        loop(nz, wait_idx)
        lax.fori_loop(0, batches, lambda b, carry: (score([choose(2 * b), choose(2 * b + 1)], 0), carry)[1], 0)

    most = pl.ds(0, n - 1)
    pltpu.make_async_copy(ret.at[most], ret.at[most], recv_r).wait()

    lane = lax.broadcasted_iota(jnp.int32, (8, 128), 1)
    columns = []
    for d in range(0, n, QUAD):
        tiles = [ret[d + t] for t in range(QUAD)]
        parts = []
        for g in range(QUAD):
            part = jnp.zeros((8, 128), jnp.float32)
            for t in range(QUAD):
                shift = (slots * (t - g)) % 128
                moved = pltpu.roll(tiles[t], shift, axis=1) if shift else tiles[t]
                part = jnp.where(lane // slots == t, moved, part)
            parts.append(part)
        columns.append(jnp.concatenate(parts, axis=0))
    back = jnp.concatenate(columns, axis=1)
    head = back.astype(jnp.bfloat16)
    tail = (back - head.astype(jnp.float32)).astype(jnp.bfloat16)
    result = jnp.zeros(out_ref.shape, jnp.float32)
    owners = owner.shape[0]
    for term in (head, tail):
        for k in range(owners):
            spread = jnp.concatenate(
                [term if j == k else jnp.zeros_like(term) for j in range(owners)], axis=0
            )
            result += lax.dot_general(pick[k], spread, NT, preferred_element_type=jnp.float32)
    out_ref[...] = result

    for sent, sem in ((idx, send_i), (gath, send_q), (stage, send_r)):
        pltpu.make_async_copy(sent.at[most], sent.at[most], sem).wait()


def on_device(n, queries, beam_owner, beam_local, leaf_weight, leaf_bias, cluster_weight, block_size):
    rows, features = queries.shape
    owners = beam_owner.shape[1]
    clusters, labels, _ = leaf_weight.shape
    slots = max(32, 2 * rows * owners // n)
    assert slots == 32 and rows == 64 and 2 * labels * owners == 128 and n % 8 == 0
    nx = chips_along_x(n)
    nz = n // (2 * nx)
    vmem = pl.BlockSpec(memory_space=pltpu.VMEM)
    hbm = pl.BlockSpec(memory_space=pltpu.HBM)
    dma = pltpu.SemaphoreType.DMA
    return pl.pallas_call(
        functools.partial(kernel, n, nx, slots, 4),
        out_shape=jax.ShapeDtypeStruct((rows, 2 * labels * owners), jnp.float32),
        in_specs=[hbm] * 7,
        out_specs=vmem,
        scratch_shapes=[
            pltpu.VMEM((n, rows, features), queries.dtype),
            pltpu.VMEM((n, owners, 128), jnp.int32),
            pltpu.VMEM((clusters * labels, features), leaf_weight.dtype),
            pltpu.VMEM((clusters, features), cluster_weight.dtype),
            pltpu.VMEM((2, 2 * QUAD * slots, features), jnp.bfloat16),
            pltpu.VMEM((n, 8, 128), jnp.float32),
            pltpu.VMEM((n, 8, 128), jnp.float32),
            pltpu.VMEM((owners, rows, n * slots), jnp.bfloat16),
            pltpu.VMEM((owners, rows), jnp.int32),
            pltpu.VMEM((2 * owners, rows), jnp.int32),
            pltpu.VMEM((labels, clusters), jnp.float32),
            pltpu.VMEM((1, clusters), jnp.int32),
            pltpu.VMEM((4 * labels, clusters), jnp.bfloat16),
            dma, dma, dma((nz,)), dma, dma,
            dma((nz * 4,)), dma((nz * (nx - 1) * 4,)), dma((nz,)), dma((nz,)), dma((nz * (nx - 1),)), dma((7,)),
        ],
        compiler_params=pltpu.CompilerParams(
            collective_id=0, has_side_effects=True, vmem_limit_bytes=56 * 2**20
        ),
    )(
        queries,
        beam_owner.T,
        beam_local.T,
        leaf_weight.reshape(clusters * labels, features),
        leaf_bias.T,
        cluster_weight,
        block_size.reshape(1, clusters),
    )


def solution(mesh):
    spec = P(("groups", "wide"))
    return jax.shard_map(
        functools.partial(on_device, mesh.shape["wide"]),
        mesh=mesh,
        in_specs=(spec,) * 7,
        out_specs=spec,
        check_vma=False,
    )
```

```python
import functools

import jax
import jax.numpy as jnp
from jax import lax
from jax.experimental import pallas as pl
from jax.experimental.pallas import tpu as pltpu
from jax.sharding import PartitionSpec as P

MESH = pl.DeviceIdType.MESH
NT = (((1,), (1,)), ((), ()))
QUAD = 4
SMALL = 16


def loop(count, body):
    if count <= SMALL:
        for step in range(count):
            body(step)
    else:
        lax.fori_loop(0, count, lambda step, carry: (body(step), carry)[1], 0)


def chips_along_x(devices):
    x = 1
    while 8 * x * x <= devices // 2:
        x *= 2
    return x


def kernel(
    n, nx, slots, pieces,
    q_hbm, owner_hbm, local_hbm, w_hbm, bias_hbm, cw_hbm, size_hbm,
    out_ref,
    gath, idx, w, cw, xc, stage, ret, pick, owner_ref, local_ref, bias_ref, size_ref, table,
    send_q, send_i, recv_i, send_r, recv_r, recv_z, recv_x, recv_c, recv_zi, recv_xi, load_sem,
):
    rows, features = q_hbm.shape
    clusters = cw_hbm.shape[0]
    labels = w_hbm.shape[0] // clusters
    pair = 2 * labels
    nz = n // (2 * nx)
    quads_per_plane = nx // 2
    piece = rows // pieces
    me = lax.axis_index("wide")
    core = lax.rem(me, 2)
    x = lax.rem(me // 2, nx)
    z = me // (2 * nx)

    def index_of(z_, x_, core_):
        return (z_ * nx + x_) * 2 + core_

    def plane(k):
        other, bit = 0, 1
        while bit < nz:
            mine, turned = lax.rem(z // bit, 2), k // bit % 2
            other = other + bit * (mine + turned - 2 * mine * turned)
            bit *= 2
        return other

    barrier = pltpu.get_barrier_semaphore()

    def greet(target):
        pl.semaphore_signal(barrier, inc=1, device_id={"wide": target}, device_id_type=MESH)

    loop(nz - 1, lambda step: greet(index_of(plane(step + 1), x, core)))
    loop(nx - 1, lambda step: greet(index_of(z, lax.rem(x + 1 + step, nx), core)))
    greet(index_of(z, x, 1 - core))

    loads = [
        pltpu.make_async_copy(source, target, load_sem.at[i])
        for i, (source, target) in enumerate([
            (owner_hbm, owner_ref), (local_hbm, local_ref), (q_hbm, gath.at[me]),
            (size_hbm, size_ref), (bias_hbm, bias_ref), (cw_hbm, cw), (w_hbm, w),
        ])
    ]
    for load in loads:
        load.start()
    owner_copy, local_copy, own_copy, size_copy, bias_copy, cw_copy, w_copy = loads
    owner_copy.wait()
    local_copy.wait()

    owner = owner_ref[...]
    local = local_ref[...]
    named = jnp.concatenate(
        [owner[k // 2:k // 2 + 1] * clusters + local[k:k + 1] for k in range(local.shape[0])], axis=0
    )
    half_beams = local.shape[0] // 2
    idx[me] = jnp.concatenate([named[:half_beams], named[half_beams:]], axis=1)

    own_copy.wait()
    pl.semaphore_wait(barrier, nz + nx - 1)

    def send_idx(number, recv, target):
        pltpu.make_async_remote_copy(
            src_ref=idx.at[number], dst_ref=idx.at[number], send_sem=send_i, recv_sem=recv,
            device_id={"wide": target}, device_id_type=MESH,
        ).start()

    def wait_one(ref, sem):
        pltpu.make_async_copy(ref, ref, sem).wait()

    def part(number, p):
        return gath.at[number, pl.ds(p * piece, piece)]

    def send(source, number, p, recv, target):
        pltpu.make_async_remote_copy(
            src_ref=source, dst_ref=part(number, p), send_sem=send_q, recv_sem=recv,
            device_id={"wide": target}, device_id_type=MESH,
        ).start()

    def to_column(k, p):
        if p == 0:
            send_idx(me, recv_zi.at[k], index_of(plane(k), x, core))
        send(own_part(p), me, p, recv_z.at[k * pieces + p], index_of(plane(k), x, core))

    def to_row(source, number, k, p):
        def one(step):
            other = lax.rem(x + 1 + step, nx)
            if p == 0:
                send_idx(number, recv_xi.at[k * (nx - 1) + step], index_of(z, other, core))
            send(source, number, p, recv_x.at[(k * (nx - 1) + step) * pieces + p], index_of(z, other, core))
        loop(nx - 1, one)

    def to_sibling(source, number, k, p):
        if p == 0:
            send_idx(number, recv_i.at[k], index_of(z, x, 1 - core))
        send(source, number, p, recv_c.at[k], index_of(z, x, 1 - core))

    def all_to_sibling(number, k):
        send_idx(number, recv_i.at[k], index_of(z, x, 1 - core))
        pltpu.make_async_remote_copy(
            src_ref=gath.at[number], dst_ref=gath.at[number], send_sem=send_q, recv_sem=recv_c.at[k],
            device_id={"wide": index_of(z, x, 1 - core)}, device_id_type=MESH,
        ).start()

    def own_part(p):
        return part(me, p)

    def from_column(k, pass_on=False):
        number = index_of(plane(k), x, core)
        wait_one(idx.at[number], recv_zi.at[k])
        for p in range(pieces):
            pltpu.make_async_copy(part(number, p), part(number, p), recv_z.at[k * pieces + p]).wait()
            to_row(part(number, p), number, k, p)
            if pass_on:
                @pl.when(middle)
                def _():
                    if p == 0:
                        send_idx(number, recv_zi.at[2], index_of(plane(1), x, core))
                    send(part(number, p), number, p, recv_z.at[2 * pieces + p], index_of(plane(1), x, core))
        all_to_sibling(number, k)

    def from_row(k, split=False):
        def one(step):
            number = index_of(plane(k), lax.rem(x + nx - 1 - step, nx), core)
            wait_one(idx.at[number], recv_xi.at[k * (nx - 1) + step])
            for p in range(pieces):
                recv = recv_x.at[(k * (nx - 1) + step) * pieces + p]
                pltpu.make_async_copy(part(number, p), part(number, p), recv).wait()
                if split:
                    to_sibling(part(number, p), number, k, p)
            if not split:
                all_to_sibling(number, k)
        loop(nx - 1, one)

    def from_sibling(k):
        some = gath.at[pl.ds(0, nx)]
        pltpu.make_async_copy(some, some, recv_c.at[k]).wait()

    relayed = n <= SMALL and nx == 2 and nz == 4
    middle = (z == 1) | (z == 2)

    def relay_order(step):
        return jnp.where(middle, (3, 1, 2)[step], step + 1)

    order = [0] + [relay_order(step) for step in range(3)]

    if not relayed:
        for p in range(pieces):
            to_row(own_part(p), me, 0, p)
    if relayed:
        for p in range(pieces):
            to_column(1, p)
            to_row(own_part(p), me, 0, p)

            @pl.when(middle)
            def _():
                to_column(3, p)

        @pl.when(jnp.logical_not(middle))
        def _():
            for k in (2, 3):
                for p in range(pieces):
                    to_column(k, p)
    else:
        loop(nz - 1, lambda step: [to_column(step + 1, p) for p in range(pieces)])
    all_to_sibling(me, 0)

    def make_table():
        size_copy.wait()
        bias_copy.wait()
        bias = bias_ref[...]
        hi = bias.astype(jnp.bfloat16)
        rest = bias - hi.astype(jnp.float32)
        mid = rest.astype(jnp.bfloat16)
        low = (rest - mid.astype(jnp.float32)).astype(jnp.bfloat16)
        size = jnp.broadcast_to(size_ref[...].astype(jnp.float32), (labels, clusters))
        table[...] = jnp.concatenate([hi, mid, low, size.astype(jnp.bfloat16)], axis=0)

    def prepare_pick():
        dev = lax.broadcasted_iota(jnp.int32, (n, rows), 0)
        hits = [owner[k:k + 1] == dev for k in range(owner.shape[0])]
        any_hit = functools.reduce(jnp.logical_or, hits)
        before = (
            lax.broadcasted_iota(jnp.int32, (rows, rows), 0)
            < lax.broadcasted_iota(jnp.int32, (rows, rows), 1)
        )
        rank = jnp.dot(
            any_hit.astype(jnp.bfloat16), before.astype(jnp.bfloat16),
            preferred_element_type=jnp.float32,
        )
        places = [
            jnp.sum(jnp.where(hit, rank, 0.0), axis=0, keepdims=True)
            + (owner[k:k + 1] * slots).astype(jnp.float32)
            for k, hit in enumerate(hits)
        ]
        place = jnp.concatenate(places + [jnp.zeros((8 - len(places), rows), jnp.float32)], axis=0)
        place = jnp.concatenate([place, jnp.zeros((8, 128 - rows), jnp.float32)], axis=1)
        place = place.T.astype(jnp.int32)
        lane = lax.broadcasted_iota(jnp.int32, (rows, n * slots), 1)
        for k in range(owner.shape[0]):
            pick[k] = (place[:rows, k:k + 1] == lane).astype(jnp.bfloat16)

    width = QUAD * rows

    def quad_number(position):
        if relayed:
            return plane(order[position])
        return plane(position // quads_per_plane) * quads_per_plane + position % quads_per_plane

    def choose(position):
        first = QUAD * quad_number(position)
        lane = lax.broadcasted_iota(jnp.int32, (half_beams, 128), 1)
        row = lax.broadcasted_iota(jnp.int32, (2 * half_beams, 128), 0)
        parts = []
        for p in range(QUAD // 2):
            left, right = idx[first + 2 * p], idx[first + 2 * p + 1]
            ids = jnp.concatenate([
                jnp.where(lane < rows, left, pltpu.roll(right, rows, axis=1)),
                jnp.where(lane < rows, pltpu.roll(left, rows, axis=1), right),
            ], axis=0)
            ids = ids - me * clusters
            inside = (ids >= 0) & (ids < clusters)
            value = jnp.where(inside, ids, 0).astype(jnp.float32)
            even = lax.rem(row, 2) == 0
            c0 = jnp.sum(jnp.where(even, value, 0.0), axis=0, keepdims=True)
            c1 = jnp.sum(jnp.where(even, 0.0, value), axis=0, keepdims=True)
            hit = jnp.sum(jnp.where(even & inside, 1.0, 0.0), axis=0, keepdims=True)
            parts.append((c0, c1, hit))
        c0, c1, hit = [jnp.concatenate(v, axis=1) for v in zip(*parts)]
        qa = lax.broadcasted_iota(jnp.int32, (width, width), 0)
        qb = lax.broadcasted_iota(jnp.int32, (width, width), 1)
        before = ((qa < qb) & (qa // rows == qb // rows)).astype(jnp.bfloat16)
        rank = jnp.dot(
            jnp.broadcast_to(hit, (8, width)).astype(jnp.bfloat16), before,
            preferred_element_type=jnp.float32,
        )[:1].astype(jnp.int32)
        lane = lax.broadcasted_iota(jnp.int32, (1, width), 1)
        place = jnp.where(hit > 0.5, rank + lane // rows * slots, -1)
        taken = (
            place == lax.broadcasted_iota(jnp.int32, (QUAD * slots, width), 0)
        ).astype(jnp.bfloat16)
        row = lax.broadcasted_iota(jnp.int32, (8, width), 0)
        both = jnp.where(row == 0, c0, jnp.where(row == 1, c1, 0.0)).astype(jnp.bfloat16)
        chosen = lax.dot_general(both, taken, NT, preferred_element_type=jnp.float32)
        return first, taken, chosen[0:1], chosen[1:2]

    def pack(pick, slot_of, place):
        first, taken, _, _ = pick
        embedded = gath[pl.ds(first, QUAD)].reshape(width, features)
        packed = jnp.dot(taken, embedded, preferred_element_type=jnp.float32)
        xc[slot_of, place * QUAD * slots:(place + 1) * QUAD * slots] = packed.astype(jnp.bfloat16)

    def score(picks, slot_of, ready=0):
        lanes = QUAD * slots * len(picks)
        for place in range(ready, len(picks)):
            pack(picks[place], slot_of, place)
        ids = [jnp.concatenate([v[2 + k] for v in picks], axis=1).astype(jnp.int32) for k in range(2)]
        x_rows = xc[slot_of, :lanes]
        wide_ids = [jnp.broadcast_to(v, (labels, lanes)) for v in ids]
        logit = [jnp.zeros((labels, lanes), jnp.float32) for _ in ids]
        step = min(16, clusters)
        for start in range(0, clusters, step):
            block = lax.dot_general(
                w[start * labels:(start + step) * labels], x_rows, NT,
                preferred_element_type=jnp.float32,
            )
            for c in range(step):
                piece = block[c * labels:(c + 1) * labels]
                logit = [jnp.where(v == start + c, piece, a) for v, a in zip(wide_ids, logit)]
        product = lax.dot_general(cw[...], x_rows, NT, preferred_element_type=jnp.float32)
        number = lax.broadcasted_iota(jnp.int32, (clusters, lanes), 0)
        scores = []
        for v, a in zip(ids, logit):
            hot = number == v
            parent = jnp.sum(jnp.where(hot, product, 0.0), axis=0, keepdims=True)
            extra = jnp.dot(table[...], hot.astype(jnp.bfloat16), preferred_element_type=jnp.float32)
            b = extra[:labels] + extra[labels:2 * labels] + extra[2 * labels:3 * labels]
            used = extra[3 * labels:]
            slot = lax.broadcasted_iota(jnp.int32, (labels, lanes), 0).astype(jnp.float32)
            value = jax.nn.sigmoid(parent) * jax.nn.sigmoid(a + b)
            scores.append(jnp.where(slot < used, value, 0.0))
        scores = jnp.concatenate(scores, axis=0)
        lane = lax.broadcasted_iota(jnp.int32, (8, 128), 1)
        for half, (first, _, _, _) in enumerate(picks):
            for t in range(QUAD):
                tile = jnp.zeros((8, 128), jnp.float32)
                for g in range(QUAD):
                    part = scores[8 * g:8 * g + 8, half * 128:half * 128 + 128]
                    shift = (slots * (g - t)) % 128
                    if shift:
                        part = pltpu.roll(part, shift, axis=1)
                    tile = jnp.where(lane // slots == g, part, tile)
                stage[first + t] = tile
        for first, _, _, _ in picks[::-1]:
            for t in range(QUAD):
                target = first + t

                @pl.when(target != me)
                def _():
                    pltpu.make_async_remote_copy(
                        src_ref=stage.at[target], dst_ref=ret.at[me],
                        send_sem=send_r, recv_sem=recv_r,
                        device_id={"wide": target}, device_id_type=MESH,
                    ).start()

                @pl.when(target == me)
                def _():
                    ret[me] = stage[me]

    batches = n // (2 * QUAD)

    def wait_idx(k):
        wait_one(idx.at[pl.ds(0, nx)], recv_i.at[k])

    prepare_pick()
    make_table()
    if relayed:
        from_column(order[1], pass_on=True)
        from_row(order[0])
        from_column(order[2])
        from_row(order[1])
        from_column(order[3])
        from_row(order[2])
        from_sibling(order[0])
        from_sibling(order[1])
        w_copy.wait()
        cw_copy.wait()
        wait_idx(order[0])
        wait_idx(order[1])
        score([choose(0), choose(1)], 0)
        wait_idx(order[2])
        picks = [choose(2)]
        from_row(order[3], split=True)
        wait_idx(order[3])
        picks.append(choose(3))
        from_sibling(order[2])
        pack(picks[0], 1, 0)
        from_sibling(order[3])
        score(picks, 1, ready=1)
    else:
        from_row(0)

        def relay(step):
            from_column(step + 1)
            from_row(step + 1)

        loop(nz - 1, relay)
        loop(nz, from_sibling)
        w_copy.wait()
        cw_copy.wait()
        loop(nz, wait_idx)
        lax.fori_loop(0, batches, lambda b, carry: (score([choose(2 * b), choose(2 * b + 1)], 0), carry)[1], 0)

    most = pl.ds(0, n - 1)
    pltpu.make_async_copy(ret.at[most], ret.at[most], recv_r).wait()

    lane = lax.broadcasted_iota(jnp.int32, (8, 128), 1)
    columns = []
    for d in range(0, n, QUAD):
        tiles = [ret[d + t] for t in range(QUAD)]
        parts = []
        for g in range(QUAD):
            part = jnp.zeros((8, 128), jnp.float32)
            for t in range(QUAD):
                shift = (slots * (t - g)) % 128
                moved = pltpu.roll(tiles[t], shift, axis=1) if shift else tiles[t]
                part = jnp.where(lane // slots == t, moved, part)
            parts.append(part)
        columns.append(jnp.concatenate(parts, axis=0))
    back = jnp.concatenate(columns, axis=1)
    head = back.astype(jnp.bfloat16)
    tail = (back - head.astype(jnp.float32)).astype(jnp.bfloat16)
    result = jnp.zeros(out_ref.shape, jnp.float32)
    owners = owner.shape[0]
    for term in (head, tail):
        for k in range(owners):
            spread = jnp.concatenate(
                [term if j == k else jnp.zeros_like(term) for j in range(owners)], axis=0
            )
            result += lax.dot_general(pick[k], spread, NT, preferred_element_type=jnp.float32)
    out_ref[...] = result

    for sent, sem in ((idx, send_i), (gath, send_q), (stage, send_r)):
        pltpu.make_async_copy(sent.at[most], sent.at[most], sem).wait()


def on_device(n, queries, beam_owner, beam_local, leaf_weight, leaf_bias, cluster_weight, block_size):
    rows, features = queries.shape
    owners = beam_owner.shape[1]
    clusters, labels, _ = leaf_weight.shape
    slots = max(32, 2 * rows * owners // n)
    assert slots == 32 and rows == 64 and 2 * labels * owners == 128 and n % 8 == 0
    nx = chips_along_x(n)
    nz = n // (2 * nx)
    vmem = pl.BlockSpec(memory_space=pltpu.VMEM)
    hbm = pl.BlockSpec(memory_space=pltpu.HBM)
    dma = pltpu.SemaphoreType.DMA
    return pl.pallas_call(
        functools.partial(kernel, n, nx, slots, 4),
        out_shape=jax.ShapeDtypeStruct((rows, 2 * labels * owners), jnp.float32),
        in_specs=[hbm] * 7,
        out_specs=vmem,
        scratch_shapes=[
            pltpu.VMEM((n, rows, features), queries.dtype),
            pltpu.VMEM((n, owners, 128), jnp.int32),
            pltpu.VMEM((clusters * labels, features), leaf_weight.dtype),
            pltpu.VMEM((clusters, features), cluster_weight.dtype),
            pltpu.VMEM((2, 2 * QUAD * slots, features), jnp.bfloat16),
            pltpu.VMEM((n, 8, 128), jnp.float32),
            pltpu.VMEM((n, 8, 128), jnp.float32),
            pltpu.VMEM((owners, rows, n * slots), jnp.bfloat16),
            pltpu.VMEM((owners, rows), jnp.int32),
            pltpu.VMEM((2 * owners, rows), jnp.int32),
            pltpu.VMEM((labels, clusters), jnp.float32),
            pltpu.VMEM((1, clusters), jnp.int32),
            pltpu.VMEM((4 * labels, clusters), jnp.bfloat16),
            dma, dma, dma((nz,)), dma, dma,
            dma((nz * 4,)), dma((nz * (nx - 1) * 4,)), dma((nz,)), dma((nz,)), dma((nz * (nx - 1),)), dma((7,)),
        ],
        compiler_params=pltpu.CompilerParams(
            collective_id=0, has_side_effects=True, vmem_limit_bytes=56 * 2**20
        ),
    )(
        queries,
        beam_owner.T,
        beam_local.T,
        leaf_weight.reshape(clusters * labels, features),
        leaf_bias.T,
        cluster_weight,
        block_size.reshape(1, clusters),
    )


def solution(mesh):
    spec = P(("groups", "wide"))
    return jax.shard_map(
        functools.partial(on_device, mesh.shape["wide"]),
        mesh=mesh,
        in_specs=(spec,) * 7,
        out_specs=spec,
        check_vma=False,
    )
```
